32 devices in a mesh: dp: 8 (over z, x), tx: 2 (over core), ty: 2 (over y).
Axes of the slice: x: 2, y: 2, z: 4, core: 2. Of those that a mesh axis runs over, the one named last changes fastest.
Arguments:
- tokens: bfloat16 [16384, 640], P(('dp', 'tx'), 'ty'), may hold values from -6 to 6
- cotangent: bfloat16 [16384, 640], P(('dp', 'tx'), 'ty'), may hold values from -6 to 6
- entry_gain: float32 [640], P('ty'), may hold values from -0.5 to 0.5
- query_weight: bfloat16 [640, 1024], P('ty', 'tx'), may hold values from -0.25 to 0.25
- key_weight: bfloat16 [640, 256], P('ty', 'tx'), may hold values from -0.25 to 0.25
- value_weight: bfloat16 [640, 256], P('ty', 'tx'), may hold values from -0.25 to 0.25
- query_scale: float32 [256], replicated, may hold values from -0.5 to 0.5
- key_scale: float32 [256], replicated, may hold values from -0.5 to 0.5
- output_weight: bfloat16 [1024, 640], P('tx', 'ty'), may hold values from -0.1875 to 0.1875
- mixed_gain: float32 [640], P('ty'), may hold values from -0.5 to 0.5
- feed_gain: float32 [640], P('ty'), may hold values from -0.5 to 0.5
- gate_weight: bfloat16 [640, 2048], P('ty', 'tx'), may hold values from -0.25 to 0.25
- up_weight: bfloat16 [640, 2048], P('ty', 'tx'), may hold values from -0.25 to 0.25
- down_weight: bfloat16 [2048, 640], P('tx', 'ty'), may hold values from -0.125 to 0.125
- final_gain: float32 [640], P('ty'), may hold values from -0.5 to 0.5
Outputs:
- block_output: bfloat16 [16384, 640], P(('dp', 'tx'), 'ty')
- tokens_gradient: float32 [16384, 640], P(('dp', 'tx'), 'ty')
- entry_gain_gradient: float32 [640], P('ty')
- query_weight_gradient: float32 [640, 1024], P('ty', 'tx')
- key_weight_gradient: float32 [640, 256], P('ty', 'tx')
- value_weight_gradient: float32 [640, 256], P('ty', 'tx')
- query_scale_gradient: float32 [256], replicated
- key_scale_gradient: float32 [256], replicated
- output_weight_gradient: float32 [1024, 640], P('tx', 'ty')
- mixed_gain_gradient: float32 [640], P('ty')
- feed_gain_gradient: float32 [640], P('ty')
- gate_weight_gradient: float32 [640, 2048], P('ty', 'tx')
- up_weight_gradient: float32 [640, 2048], P('ty', 'tx')
- down_weight_gradient: float32 [2048, 640], P('tx', 'ty')
- final_gain_gradient: float32 [640], P('ty')
The draws below stay inside these ranges and needn't reach their ends.
All inputs are finite; a program needn't handle non-finite values.
Results may differ from the reference program's by a relative error of at most 0.018.
Values may be sent and summed in bfloat16 or wider, within the bound.
A program may use at most 128 MiB of HBM per device.

```python
import jax
import jax.numpy as jnp
from jax import lax

D = 640
HEADS = 4
HEAD_DIM = 256
FF = 2048
WINDOW = 512
LEN = 2048
TOKENS = 16384
N_DP = 8


def block_scale(key, extent, pieces, least, top_value):
    level = 1.0
    for position, shards_of in pieces:
        steps = jax.random.uniform(jax.random.fold_in(jax.random.fold_in(key, 6), position), (shards_of,), jnp.float32, least / len(pieces), top_value / len(pieces))
        level = level * jnp.repeat(jnp.exp(steps), extent[position] // shards_of).reshape((-1,) + (1,) * (len(extent) - 1 - position))
    return level


def noise(own_key, extent, spread, most, split=(), held_as=jnp.bfloat16):
    drawn = spread * jax.random.normal(own_key, extent, jnp.float32)
    if split:
        drawn = drawn * block_scale(own_key, extent, split, -0.22, 0.18)
    return jnp.clip(drawn, -most, most).astype(held_as)


def setup_inputs(seed: int = 0) -> dict:
    key_of = jax.random.split(jax.random.key(seed), 16)
    tokens = noise(key_of[0], (TOKENS, D), 1.0, 6.0, ((0, 16), (1, 2)))
    cotangent = noise(key_of[1], (TOKENS, D), 1.0, 6.0, ((0, 16), (1, 2)))
    entry_gain = jnp.clip(jax.random.uniform(key_of[2], (D,), jnp.float32, -0.5, 0.5) * block_scale(key_of[2], (D,), ((0, 2),), -0.4, 0.0), -0.5, 0.5)
    query_weight = noise(key_of[3], (D, HEADS * HEAD_DIM), D ** -0.5, 0.25, ((0, 2), (1, 2)))
    key_weight = noise(key_of[4], (D, HEAD_DIM), D ** -0.5, 0.25, ((0, 2), (1, 2)))
    value_weight = noise(key_of[5], (D, HEAD_DIM), D ** -0.5, 0.25, ((0, 2), (1, 2)))
    query_scale = jnp.clip(jax.random.uniform(key_of[6], (HEAD_DIM,), jnp.float32, -0.5, 0.5), -0.5, 0.5)
    key_scale = jnp.clip(jax.random.uniform(key_of[7], (HEAD_DIM,), jnp.float32, -0.5, 0.5), -0.5, 0.5)
    output_weight = noise(key_of[8], (HEADS * HEAD_DIM, D), (HEADS * HEAD_DIM) ** -0.5, 0.1875, ((0, 2), (1, 2)))
    mixed_gain = jnp.clip(jax.random.uniform(key_of[9], (D,), jnp.float32, -0.5, 0.5) * block_scale(key_of[9], (D,), ((0, 2),), -0.4, 0.0), -0.5, 0.5)
    feed_gain = jnp.clip(jax.random.uniform(key_of[10], (D,), jnp.float32, -0.5, 0.5) * block_scale(key_of[10], (D,), ((0, 2),), -0.4, 0.0), -0.5, 0.5)
    gate_weight = noise(key_of[11], (D, FF), D ** -0.5, 0.25, ((0, 2), (1, 2)))
    up_weight = noise(key_of[12], (D, FF), D ** -0.5, 0.25, ((0, 2), (1, 2)))
    down_weight = noise(key_of[13], (FF, D), FF ** -0.5, 0.125, ((0, 2), (1, 2)))
    final_gain = jnp.clip(jax.random.uniform(key_of[14], (D,), jnp.float32, -0.5, 0.5) * block_scale(key_of[14], (D,), ((0, 2),), -0.4, 0.0), -0.5, 0.5)
    return dict(tokens=tokens, cotangent=cotangent, entry_gain=entry_gain, query_weight=query_weight, key_weight=key_weight, value_weight=value_weight, query_scale=query_scale, key_scale=key_scale, output_weight=output_weight, mixed_gain=mixed_gain, feed_gain=feed_gain, gate_weight=gate_weight, up_weight=up_weight, down_weight=down_weight, final_gain=final_gain)


EPS = 1e-06
MASKED = -1e+30
HIGHEST = lax.Precision.HIGHEST

@jax.custom_vjp
def low(v):
    return lax.optimization_barrier(v.astype(jnp.bfloat16)).astype(jnp.float32)

@jax.custom_vjp
def low_back(v):
    return v

def low_keep(v):
    return (low(v), None)

def low_pass(kept, grad):
    return (grad,)

def back_keep(v):
    return (v, None)

def back_low(kept, grad):
    return (low(grad),)
low.defvjp(low_keep, low_pass)
low_back.defvjp(back_keep, back_low)

def root_norm(value, gain):
    factor = lax.rsqrt(lax.optimization_barrier(jnp.mean(value * value, axis=-1, keepdims=True)) + EPS)
    return value * factor * (1.0 + gain)

def rotary_tables(places):
    half = HEAD_DIM // 2
    inverse = 10000.0 ** (-(jnp.arange(half, dtype=jnp.float32) * 2.0) / HEAD_DIM)
    angles = places.astype(jnp.float32)[:, None] * inverse[None, :]
    return (jnp.cos(angles)[:, None, :], jnp.sin(angles)[:, None, :])

def rotate(value, cosine, sine):
    half = value.shape[-1] // 2
    first = value[..., :half]
    second = value[..., half:]
    return jnp.concatenate([first * cosine - second * sine, second * cosine + first * sine], axis=-1)

def window_mask(start, window):
    rows_place = start + jnp.arange(window, dtype=jnp.int32)
    cols_place = start - window + jnp.arange(2 * window, dtype=jnp.int32)
    return (cols_place[None, :] >= 0) & (cols_place[None, :] <= rows_place[:, None]) & (rows_place[:, None] - cols_place[None, :] < window)

def gated_gelu(gate, upper):
    return jax.nn.gelu(gate, approximate=True) * upper

def attend(query, keys, values):
    zero_rows = jnp.zeros((WINDOW, HEAD_DIM), keys.dtype)
    keys_padded = jnp.concatenate([zero_rows, keys], axis=0)
    values_padded = jnp.concatenate([zero_rows, values], axis=0)

    def block(index):
        start = index * WINDOW
        query_block = lax.dynamic_slice_in_dim(query, start, WINDOW, 0)
        key_block = lax.dynamic_slice_in_dim(keys_padded, start, 2 * WINDOW, 0)
        value_block = lax.dynamic_slice_in_dim(values_padded, start, 2 * WINDOW, 0)
        scores = low_back(jnp.einsum('qhd,kd->hqk', query_block, key_block, precision=HIGHEST) * HEAD_DIM ** (-0.5))
        masked = jnp.where(window_mask(start, WINDOW)[None], scores, MASKED)
        shares = low(jax.nn.softmax(masked, axis=-1))
        return jnp.einsum('hqk,kd->qhd', shares, value_block, precision=HIGHEST)
    blocks = lax.map(jax.checkpoint(block), jnp.arange(LEN // WINDOW, dtype=jnp.int32))
    return blocks.reshape(LEN, HEADS * HEAD_DIM)

def layer(sequence, params):
    entry_gain, query_weight, key_weight, value_weight, query_scale, key_scale, output_weight, mixed_gain, feed_gain, gate_weight, up_weight, down_weight, final_gain = params
    normed = low(root_norm(sequence, entry_gain))
    query_raw = low_back(jnp.dot(normed, query_weight, precision=HIGHEST))
    key_raw = low_back(jnp.dot(normed, key_weight, precision=HIGHEST))
    value_raw = low_back(jnp.dot(normed, value_weight, precision=HIGHEST))
    cosine, sine = rotary_tables(jnp.arange(LEN, dtype=jnp.int32))
    query = low(rotate(root_norm(query_raw.reshape(LEN, HEADS, HEAD_DIM), query_scale), cosine, sine))
    keys = low(rotate(root_norm(key_raw[:, None, :], key_scale), cosine, sine)[:, 0, :])
    values = low(value_raw)
    attended = low(low_back(attend(query, keys, values)))
    mixed = low_back(jnp.dot(attended, output_weight, precision=HIGHEST))
    hidden = sequence + root_norm(mixed, mixed_gain)
    fed = low(root_norm(hidden, feed_gain))
    gate = low_back(jnp.dot(fed, gate_weight, precision=HIGHEST))
    upper = low_back(jnp.dot(fed, up_weight, precision=HIGHEST))
    inner = low(gated_gelu(gate, upper))
    down = low_back(jnp.dot(inner, down_weight, precision=HIGHEST))
    return hidden + root_norm(down, final_gain)

def reference(tokens, cotangent, entry_gain, query_weight, key_weight, value_weight, query_scale, key_scale, output_weight, mixed_gain, feed_gain, gate_weight, up_weight, down_weight, final_gain):
    params = (entry_gain.astype(jnp.float32), query_weight.astype(jnp.float32), key_weight.astype(jnp.float32), value_weight.astype(jnp.float32), query_scale.astype(jnp.float32), key_scale.astype(jnp.float32), output_weight.astype(jnp.float32), mixed_gain.astype(jnp.float32), feed_gain.astype(jnp.float32), gate_weight.astype(jnp.float32), up_weight.astype(jnp.float32), down_weight.astype(jnp.float32), final_gain.astype(jnp.float32))
    sequences = tokens.astype(jnp.float32).reshape(N_DP, LEN, D)
    incoming = cotangent.astype(jnp.float32).reshape(N_DP, LEN, D)

    def step(totals, pair):
        sequence, back_seq = pair
        output, pull = jax.vjp(layer, sequence, params)
        back_tokens, back_params = pull(back_seq)
        return (jax.tree.map(jnp.add, totals, back_params), (output, back_tokens))
    zeros = jax.tree.map(jnp.zeros_like, params)
    totals, (outputs, back_all) = lax.scan(step, zeros, (sequences, incoming))
    return (outputs.reshape(TOKENS, D).astype(jnp.bfloat16), back_all.reshape(TOKENS, D), totals[0], totals[1], totals[2], totals[3], totals[4], totals[5], totals[6], totals[7], totals[8], totals[9], totals[10], totals[11], totals[12])
```

```python
from functools import partial

import jax
import jax.numpy as jnp
from jax import lax
from jax.experimental import pallas as pl
from jax.experimental.pallas import tpu as pltpu
from jax.sharding import PartitionSpec as P

HEAD_DIM = 256
WINDOW = 512
CHUNK = 128
EPS = 1e-06
MASKED = -1e30
BF = jnp.bfloat16
F32 = jnp.float32


def mm(a, b):
    return jnp.dot(a, b, preferred_element_type=F32)


def mm_nt(a, b):
    return lax.dot_general(a, b, (((1,), (1,)), ((), ())), preferred_element_type=F32)


def mm_tn(a, b):
    return lax.dot_general(a, b, (((0,), (0,)), ((), ())), preferred_element_type=F32)


def swap(value, axis):
    return lax.ppermute(value, axis, [(0, 1), (1, 0)])


def swap_dp(value, bit):
    n = lax.axis_size("dp")
    return lax.ppermute(value, "dp", [(i, i ^ (1 << bit)) for i in range(n)])


def ordered(flag, mine, other, axis=0):
    return jnp.where(
        flag == 0,
        jnp.concatenate([mine, other], axis=axis),
        jnp.concatenate([other, mine], axis=axis),
    )


def peer_block(block):
    if lax.axis_size("dp") % 2:
        return swap(block, "ty")
    odd = lax.axis_index("dp") % 2
    half = block.shape[0] // 2
    direct = swap(lax.dynamic_slice_in_dim(block, odd * half, half, 0), "ty")
    relayed = swap_dp(direct, 0)
    return ordered(odd, direct, relayed)


def rotary_tables(places):
    half = HEAD_DIM // 2
    inverse = 10000.0 ** (-(jnp.arange(half, dtype=F32) * 2.0) / HEAD_DIM)
    angles = places.astype(F32)[:, None] * inverse[None, :]
    return (jnp.cos(angles)[:, None, :], jnp.sin(angles)[:, None, :])


def rotate(value, cosine, sine):
    half = value.shape[-1] // 2
    first = value[..., :half]
    second = value[..., half:]
    return jnp.concatenate(
        [first * cosine - second * sine, second * cosine + first * sine], axis=-1
    )


def head_prepare(raw, gain, cosine, sine):
    factor = lax.rsqrt(jnp.mean(raw * raw, axis=-1, keepdims=True) + EPS)
    return rotate(raw * factor * (1.0 + gain), cosine, sine)


def gated_gelu(gate, upper):
    return jax.nn.gelu(gate, approximate=True) * upper


def norm_forward(value, gain):
    factor = lax.rsqrt(jnp.mean(value * value, axis=1, keepdims=True) + EPS)
    return (value * factor * (1.0 + gain), factor)


def norm_backward(value, factor, gain, incoming):
    weighted = incoming * (1.0 + gain)
    inner = jnp.mean(value * weighted, axis=1, keepdims=True)
    back_value = weighted * factor - value * factor**3 * inner
    back_gain = jnp.sum(incoming * value * factor, axis=0)
    return (back_value, back_gain)


def band(first_ref, start, heads):
    rows = heads * CHUNK
    span = WINDOW + CHUNK
    place = lax.broadcasted_iota(jnp.int32, (rows, span), 0) % CHUNK
    key = lax.broadcasted_iota(jnp.int32, (rows, span), 1)
    lowest = jnp.where(first_ref[0] > 0, 0, WINDOW - start)
    return (key > place) & (key <= place + WINDOW) & (key >= lowest)


def stack_heads(ref, start, heads):
    return jnp.concatenate(
        [ref[start : start + CHUNK, h * HEAD_DIM : (h + 1) * HEAD_DIM] for h in range(heads)],
        axis=0,
    )


def attend_kernel(first_ref, query_ref, keys_ref, values_ref, out_ref, logsum_ref):
    length, width = query_ref.shape
    heads = width // HEAD_DIM
    factor = HEAD_DIM ** (-0.5)
    for start in range(0, length, CHUNK):
        query = stack_heads(query_ref, start, heads)
        keys = keys_ref[start : start + WINDOW + CHUNK, :]
        values = values_ref[start : start + WINDOW + CHUNK, :]
        scores = jnp.where(band(first_ref, start, heads), mm_nt(query, keys) * factor, MASKED)
        peak = jnp.max(scores, axis=1, keepdims=True)
        raised = jnp.exp(scores - peak)
        mass = jnp.sum(raised, axis=1, keepdims=True)
        shares = (raised / mass).astype(BF)
        out = mm(shares, values).astype(BF)
        logsum_ref[start * heads : (start + CHUNK) * heads, :] = jnp.broadcast_to(
            peak + jnp.log(mass), (heads * CHUNK, 128)
        )
        for h in range(heads):
            out_ref[start : start + CHUNK, h * HEAD_DIM : (h + 1) * HEAD_DIM] = out[
                h * CHUNK : (h + 1) * CHUNK, :
            ]


def attend_back_kernel(
    first_ref, query_ref, keys_ref, values_ref, logsum_ref, back_ref, dq_ref, dk_ref, dv_ref
):
    length, width = query_ref.shape
    heads = width // HEAD_DIM
    factor = HEAD_DIM ** (-0.5)
    dk_ref[...] = jnp.zeros_like(dk_ref)
    dv_ref[...] = jnp.zeros_like(dv_ref)
    for start in range(0, length, CHUNK):
        span = slice(start, start + WINDOW + CHUNK)
        query = stack_heads(query_ref, start, heads)
        back = stack_heads(back_ref, start, heads)
        keys = keys_ref[span, :]
        values = values_ref[span, :]
        scores = jnp.where(band(first_ref, start, heads), mm_nt(query, keys) * factor, MASKED)
        logsum = logsum_ref[start * heads : (start + CHUNK) * heads, :][:, :1]
        exact = jnp.exp(scores - logsum)
        back_shares = mm_nt(back, values)
        inner = jnp.sum(exact * back_shares, axis=1, keepdims=True)
        back_scores = (exact * (back_shares - inner)).astype(BF)
        dq = mm(back_scores, keys) * factor
        dk_ref[span, :] += mm_tn(back_scores, query) * factor
        dv_ref[span, :] += mm_tn(exact.astype(BF), back)
        for h in range(heads):
            dq_ref[start : start + CHUNK, h * HEAD_DIM : (h + 1) * HEAD_DIM] = dq[
                h * CHUNK : (h + 1) * CHUNK, :
            ]


def specs(n):
    vmem = pl.BlockSpec(memory_space=pltpu.VMEM)
    return [pl.BlockSpec(memory_space=pltpu.SMEM)] + [vmem] * n


def attend(first, query, keys, values):
    length, width = query.shape
    heads = width // HEAD_DIM
    vmem = pl.BlockSpec(memory_space=pltpu.VMEM)
    return pl.pallas_call(
        attend_kernel,
        in_specs=specs(3),
        out_specs=(vmem, vmem),
        out_shape=(
            jax.ShapeDtypeStruct((length, width), BF),
            jax.ShapeDtypeStruct((length * heads, 128), F32),
        ),
        compiler_params=pltpu.CompilerParams(vmem_limit_bytes=40 * 2**20),
        cost_estimate=pl.CostEstimate(
            flops=4 * length * width * (WINDOW + CHUNK),
            bytes_accessed=6 * 2**20,
            transcendentals=length * heads * (WINDOW + CHUNK),
        ),
    )(first, query, keys, values)


def attend_back(first, query, keys, values, logsum, back):
    length, width = query.shape
    heads = width // HEAD_DIM
    vmem = pl.BlockSpec(memory_space=pltpu.VMEM)
    return pl.pallas_call(
        attend_back_kernel,
        in_specs=specs(5),
        out_specs=(vmem, vmem, vmem),
        out_shape=(
            jax.ShapeDtypeStruct((length, width), F32),
            jax.ShapeDtypeStruct(keys.shape, F32),
            jax.ShapeDtypeStruct(values.shape, F32),
        ),
        compiler_params=pltpu.CompilerParams(vmem_limit_bytes=40 * 2**20),
        cost_estimate=pl.CostEstimate(
            flops=10 * length * width * (WINDOW + CHUNK),
            bytes_accessed=8 * 2**20,
            transcendentals=length * heads * (WINDOW + CHUNK),
        ),
    )(first, query, keys, values, logsum, back)


def total_data(block, ty_last):
    count = lax.axis_size("dp")
    rows, cols = block.shape
    rows //= 2
    if count & (count - 1) or rows % count:
        kept = block[:rows] + swap(block[rows:].astype(BF), "ty").astype(F32)
        return lax.psum(kept.astype(BF), "dp").astype(F32)
    bits = list(range(count.bit_length() - 1))
    me = lax.axis_index("dp")
    own = block[:rows].reshape(count, rows // count, cols)
    peer = block[rows:].reshape(count, rows // count, cols)
    if not ty_last:
        own = own + swap(peer.astype(BF), "ty").astype(F32)
        parts = own[:, None]
    else:
        parts = jnp.stack([own, peer], axis=1)
    for bit in bits:
        half = parts.shape[0] // 2
        flag = (me >> bit) & 1
        kept = lax.dynamic_slice_in_dim(parts, flag * half, half, 0)
        sent = lax.dynamic_slice_in_dim(parts, (1 - flag) * half, half, 0).astype(BF)
        parts = kept + swap_dp(sent, bit).astype(F32)
    if ty_last:
        parts = parts[:, :1] + swap(parts[:, 1:].astype(BF), "ty").astype(F32)
    result = parts[:, 0].astype(BF)
    for bit in reversed(bits):
        result = ordered((me >> bit) & 1, result, swap_dp(result, bit))
    return result.astype(F32).reshape(rows, cols)


def core_total(mine, other):
    return mine + swap(other.astype(BF), "tx").astype(F32)


def per_device(
    tokens,
    cotangent,
    entry_gain,
    query_weight,
    key_weight,
    value_weight,
    query_scale,
    key_scale,
    output_weight,
    mixed_gain,
    feed_gain,
    gate_weight,
    up_weight,
    down_weight,
    final_gain,
):
    tx = lax.axis_index("tx")
    ty = lax.axis_index("ty")
    quarter = tx * 2 + ty
    share, width = tokens.shape
    share //= 2
    query_cols = query_weight.shape[1]
    part = key_weight.shape[1]
    hidden_cols = gate_weight.shape[1]
    places = lax.axis_size("tx") * lax.axis_size("ty")

    gains_own = jnp.stack([entry_gain, mixed_gain, feed_gain, final_gain])
    gains = jnp.concatenate([gains_own, swap(gains_own, "ty")], axis=1)

    def to_rows(array):
        mine = lax.dynamic_slice_in_dim(array, ty * share, share, 0)
        sent = lax.dynamic_slice_in_dim(array, (1 - ty) * share, share, 0)
        return jnp.concatenate([mine, swap(sent, "ty")], axis=1)

    def from_rows(array):
        return ordered(ty, array[:, :width], swap(array[:, width:], "ty"))

    residual = to_rows(tokens).astype(F32)

    def gather_rows(weight):
        mine = jnp.concatenate([weight, peer_block(weight)], axis=0)
        return mine, swap(mine, "tx")

    def gather_cols(weight):
        mine = jnp.concatenate([weight, peer_block(weight)], axis=1)
        return mine, swap(mine, "tx")

    entry_own, entry_other = gather_rows(
        jnp.concatenate([query_weight, key_weight, value_weight], axis=1)
    )
    out_own, out_other = gather_cols(output_weight)
    feed_own, feed_other = gather_rows(jnp.concatenate([gate_weight, up_weight], axis=1))
    down_own, down_other = gather_cols(down_weight)
    incoming = to_rows(cotangent).astype(F32)

    pair_own = entry_own[:, query_cols:]
    pair_other = entry_other[:, query_cols:]
    query_w = jnp.concatenate([entry_own[:, :query_cols], entry_other[:, :query_cols]], axis=1)
    key_w = ordered(tx, pair_own[:, :part], pair_other[:, :part], axis=1)
    value_w = ordered(tx, pair_own[:, part:], pair_other[:, part:], axis=1)
    pair_w = jnp.concatenate([key_w, value_w], axis=1)
    out_w = jnp.concatenate([out_own, out_other], axis=0)
    down_w = jnp.concatenate([down_own, down_other], axis=0)

    normed, factor_one = norm_forward(residual, gains[0])
    normed = normed.astype(BF)
    pair_raw = mm(normed, pair_w)
    key_raw = pair_raw[:, :HEAD_DIM]
    cosine, sine = rotary_tables(quarter * share + jnp.arange(share, dtype=jnp.int32))
    key_rot, key_pull = jax.vjp(
        partial(head_prepare, cosine=cosine, sine=sine), key_raw[:, None, :], key_scale
    )
    pair_low = jnp.concatenate([key_rot[:, 0, :], pair_raw[:, HEAD_DIM:]], axis=1).astype(BF)
    ahead = [(i, i + 1) for i in range(places - 1)]
    before = lax.ppermute(pair_low, ("tx", "ty"), ahead)
    query_raw = mm(normed, query_w)
    heads = query_raw.shape[1] // HEAD_DIM
    query_rot, query_pull = jax.vjp(
        partial(head_prepare, cosine=cosine, sine=sine),
        query_raw.reshape(share, heads, HEAD_DIM),
        query_scale,
    )
    query_low = query_rot.astype(BF).reshape(share, heads * HEAD_DIM)
    window = jnp.concatenate([before, pair_low], axis=0)
    keys, values = window[:, :HEAD_DIM], window[:, HEAD_DIM:]
    first = quarter.reshape(1).astype(jnp.int32)
    attended, logsum = attend(first, query_low, keys, values)

    mixed = mm(attended, out_w)
    mixed_normed, factor_two = norm_forward(mixed, gains[1])
    hidden = residual + mixed_normed
    fed, factor_three = norm_forward(hidden, gains[2])
    fed = fed.astype(BF)
    hc = hidden_cols
    gate_up_own = mm(fed, feed_own)
    gate_up_other = mm(fed, feed_other)
    inner_own, pull_own = jax.vjp(gated_gelu, gate_up_own[:, :hc], gate_up_own[:, hc:])
    inner_other, pull_other = jax.vjp(gated_gelu, gate_up_other[:, :hc], gate_up_other[:, hc:])
    inner_own = inner_own.astype(BF)
    inner_other = inner_other.astype(BF)
    down = mm(jnp.concatenate([inner_own, inner_other], axis=1), down_w)
    down_normed, factor_four = norm_forward(down, gains[3])
    block_output = from_rows((hidden + down_normed).astype(BF))

    back_down, final_gain_part = norm_backward(down, factor_four, gains[3], incoming)
    back_down = back_down.astype(BF)
    down_total = core_total(mm_tn(back_down, inner_own), mm_tn(back_down, inner_other))
    down_gradient = total_data(down_total, False)
    back_own = jnp.concatenate(pull_own(mm_nt(back_down, down_own)), axis=1).astype(BF)
    back_other = jnp.concatenate(pull_other(mm_nt(back_down, down_other)), axis=1).astype(BF)
    feed_total = core_total(mm_tn(fed, back_own), mm_tn(fed, back_other))
    gate_gradient = total_data(feed_total[:, :hc], True)
    up_gradient = total_data(feed_total[:, hc:], False)
    back_fed = mm_nt(back_own, feed_own) + mm_nt(back_other, feed_other)
    back_three, feed_gain_part = norm_backward(hidden, factor_three, gains[2], back_fed)
    back_hidden = incoming + back_three
    back_mixed, mixed_gain_part = norm_backward(mixed, factor_two, gains[1], back_hidden)
    back_mixed = back_mixed.astype(BF)
    qc = query_cols
    out_total = core_total(mm_tn(back_mixed, attended[:, :qc]), mm_tn(back_mixed, attended[:, qc:]))
    out_gradient = total_data(out_total, True)
    back_attended = mm_nt(back_mixed, out_w).astype(BF)
    back_query_rot, key_part, value_part = attend_back(
        first, query_low, keys, values, logsum, back_attended
    )
    back_pair = jnp.concatenate([key_part, value_part], axis=1)
    returned = lax.ppermute(
        back_pair[:WINDOW].astype(BF), ("tx", "ty"), [(j, i) for i, j in ahead]
    )
    back_query_raw, query_scale_part = query_pull(
        back_query_rot.reshape(share, heads, HEAD_DIM)
    )
    query_back = back_query_raw.reshape(share, heads * HEAD_DIM).astype(BF)
    back_pair = back_pair[WINDOW:] + returned.astype(F32)
    back_key_raw, key_scale_part = key_pull(back_pair[:, None, :HEAD_DIM])
    key_back = back_key_raw[:, 0, :].astype(BF)
    value_back = back_pair[:, HEAD_DIM:].astype(BF)

    def columns(index, block):
        return jnp.concatenate(
            [
                block,
                lax.dynamic_slice_in_dim(key_back, index * part, part, 1),
                lax.dynamic_slice_in_dim(value_back, index * part, part, 1),
            ],
            axis=1,
        )

    entry_total = core_total(
        mm_tn(normed, columns(tx, query_back[:, :qc])),
        mm_tn(normed, columns(1 - tx, query_back[:, qc:])),
    )
    entry_gradient = total_data(entry_total, False)
    back_normed = mm_nt(query_back, query_w) + mm_nt(
        jnp.concatenate([key_back, value_back], axis=1), pair_w
    )
    back_entry, entry_gain_part = norm_backward(residual, factor_one, gains[0], back_normed)
    tokens_gradient = from_rows(back_hidden + back_entry)

    gain_parts = jnp.stack([entry_gain_part, mixed_gain_part, feed_gain_part, final_gain_part])
    gain_parts = ordered(ty, gain_parts[:, :width], gain_parts[:, width:], axis=1)
    gain_totals, query_scale_gradient, key_scale_gradient = lax.psum(
        (gain_parts, query_scale_part, key_scale_part), ("dp", "tx", "ty")
    )
    mine = lax.dynamic_slice_in_dim(gain_totals, ty * width, width, 1)
    return (
        block_output,
        tokens_gradient,
        mine[0],
        entry_gradient[:, :qc],
        entry_gradient[:, qc : qc + part],
        entry_gradient[:, qc + part :],
        query_scale_gradient,
        key_scale_gradient,
        out_gradient.T,
        mine[1],
        mine[2],
        gate_gradient,
        up_gradient,
        down_gradient.T,
        mine[3],
    )


def solution(mesh):
    in_specs = (
        P(("dp", "tx"), "ty"),
        P(("dp", "tx"), "ty"),
        P("ty"),
        P("ty", "tx"),
        P("ty", "tx"),
        P("ty", "tx"),
        P(),
        P(),
        P("tx", "ty"),
        P("ty"),
        P("ty"),
        P("ty", "tx"),
        P("ty", "tx"),
        P("tx", "ty"),
        P("ty"),
    )
    out_specs = (
        P(("dp", "tx"), "ty"),
        P(("dp", "tx"), "ty"),
        P("ty"),
        P("ty", "tx"),
        P("ty", "tx"),
        P("ty", "tx"),
        P(),
        P(),
        P("tx", "ty"),
        P("ty"),
        P("ty"),
        P("ty", "tx"),
        P("ty", "tx"),
        P("tx", "ty"),
        P("ty"),
    )
    return jax.shard_map(
        per_device, mesh=mesh, in_specs=in_specs, out_specs=out_specs, check_vma=False
    )
```

```python
from functools import partial

import jax
import jax.numpy as jnp
from jax import lax
from jax.experimental import pallas as pl
from jax.experimental.pallas import tpu as pltpu
from jax.sharding import PartitionSpec as P

HEAD_DIM = 256
WINDOW = 512
CHUNK = 128
EPS = 1e-06
MASKED = -1e30
BF = jnp.bfloat16
F32 = jnp.float32


def mm(a, b):
    return jnp.dot(a, b, preferred_element_type=F32)


def mm_nt(a, b):
    return lax.dot_general(a, b, (((1,), (1,)), ((), ())), preferred_element_type=F32)


def mm_tn(a, b):
    return lax.dot_general(a, b, (((0,), (0,)), ((), ())), preferred_element_type=F32)


def swap(value, axis):
    return lax.ppermute(value, axis, [(0, 1), (1, 0)])


def swap_dp(value, bit):
    n = lax.axis_size("dp")
    return lax.ppermute(value, "dp", [(i, i ^ (1 << bit)) for i in range(n)])


def ordered(flag, mine, other, axis=0):
    return jnp.where(
        flag == 0,
        jnp.concatenate([mine, other], axis=axis),
        jnp.concatenate([other, mine], axis=axis),
    )


def half_of(block):
    half = block.shape[0] // 2
    return lax.dynamic_slice_in_dim(block, (lax.axis_index("dp") % 2) * half, half, 0)


def relay(direct):
    return ordered(lax.axis_index("dp") % 2, direct, swap_dp(direct, 0))


def rotary_tables(places):
    half = HEAD_DIM // 2
    inverse = 10000.0 ** (-(jnp.arange(half, dtype=F32) * 2.0) / HEAD_DIM)
    angles = places.astype(F32)[:, None] * inverse[None, :]
    return (jnp.cos(angles)[:, None, :], jnp.sin(angles)[:, None, :])


def rotate(value, cosine, sine):
    half = value.shape[-1] // 2
    first = value[..., :half]
    second = value[..., half:]
    return jnp.concatenate(
        [first * cosine - second * sine, second * cosine + first * sine], axis=-1
    )


def head_prepare(raw, gain, cosine, sine):
    factor = lax.rsqrt(jnp.mean(raw * raw, axis=-1, keepdims=True) + EPS)
    return rotate(raw * factor * (1.0 + gain), cosine, sine)


def gated_gelu(gate, upper):
    return jax.nn.gelu(gate, approximate=True) * upper


def norm_forward(value, gain):
    factor = lax.rsqrt(jnp.mean(value * value, axis=1, keepdims=True) + EPS)
    return (value * factor * (1.0 + gain), factor)


def norm_backward(value, factor, gain, incoming):
    weighted = incoming * (1.0 + gain)
    inner = jnp.mean(value * weighted, axis=1, keepdims=True)
    back_value = weighted * factor - value * factor**3 * inner
    back_gain = jnp.sum(incoming * value * factor, axis=0)
    return (back_value, back_gain)


def band(first_ref, start, heads):
    rows = heads * CHUNK
    span = WINDOW + CHUNK
    place = lax.broadcasted_iota(jnp.int32, (rows, span), 0) % CHUNK
    key = lax.broadcasted_iota(jnp.int32, (rows, span), 1)
    lowest = jnp.where(first_ref[0] > 0, 0, WINDOW - start)
    return (key > place) & (key <= place + WINDOW) & (key >= lowest)


def stack_heads(ref, start, heads):
    return jnp.concatenate(
        [ref[start : start + CHUNK, h * HEAD_DIM : (h + 1) * HEAD_DIM] for h in range(heads)],
        axis=0,
    )


def attend_kernel(first_ref, query_ref, keys_ref, values_ref, out_ref, logsum_ref):
    length, width = query_ref.shape
    heads = width // HEAD_DIM
    factor = HEAD_DIM ** (-0.5)
    for start in range(0, length, CHUNK):
        query = stack_heads(query_ref, start, heads)
        keys = keys_ref[start : start + WINDOW + CHUNK, :]
        values = values_ref[start : start + WINDOW + CHUNK, :]
        scores = jnp.where(band(first_ref, start, heads), mm_nt(query, keys) * factor, MASKED)
        peak = jnp.max(scores, axis=1, keepdims=True)
        raised = jnp.exp(scores - peak)
        mass = jnp.sum(raised, axis=1, keepdims=True)
        shares = (raised / mass).astype(BF)
        out = mm(shares, values).astype(BF)
        logsum_ref[start * heads : (start + CHUNK) * heads, :] = jnp.broadcast_to(
            peak + jnp.log(mass), (heads * CHUNK, 128)
        )
        for h in range(heads):
            out_ref[start : start + CHUNK, h * HEAD_DIM : (h + 1) * HEAD_DIM] = out[
                h * CHUNK : (h + 1) * CHUNK, :
            ]


def attend_back_kernel(
    first_ref, query_ref, keys_ref, values_ref, logsum_ref, back_ref, dq_ref, dk_ref, dv_ref
):
    length, width = query_ref.shape
    heads = width // HEAD_DIM
    factor = HEAD_DIM ** (-0.5)
    dk_ref[...] = jnp.zeros_like(dk_ref)
    dv_ref[...] = jnp.zeros_like(dv_ref)
    for start in range(0, length, CHUNK):
        span = slice(start, start + WINDOW + CHUNK)
        query = stack_heads(query_ref, start, heads)
        back = stack_heads(back_ref, start, heads)
        keys = keys_ref[span, :]
        values = values_ref[span, :]
        scores = jnp.where(band(first_ref, start, heads), mm_nt(query, keys) * factor, MASKED)
        logsum = logsum_ref[start * heads : (start + CHUNK) * heads, :][:, :1]
        exact = jnp.exp(scores - logsum)
        back_shares = mm_nt(back, values)
        inner = jnp.sum(exact * back_shares, axis=1, keepdims=True)
        back_scores = (exact * (back_shares - inner)).astype(BF)
        dq = mm(back_scores, keys) * factor
        dk_ref[span, :] += mm_tn(back_scores, query) * factor
        dv_ref[span, :] += mm_tn(exact.astype(BF), back)
        for h in range(heads):
            dq_ref[start : start + CHUNK, h * HEAD_DIM : (h + 1) * HEAD_DIM] = dq[
                h * CHUNK : (h + 1) * CHUNK, :
            ]


def specs(n):
    vmem = pl.BlockSpec(memory_space=pltpu.VMEM)
    return [pl.BlockSpec(memory_space=pltpu.SMEM)] + [vmem] * n


def attend(first, query, keys, values):
    length, width = query.shape
    heads = width // HEAD_DIM
    vmem = pl.BlockSpec(memory_space=pltpu.VMEM)
    return pl.pallas_call(
        attend_kernel,
        in_specs=specs(3),
        out_specs=(vmem, vmem),
        out_shape=(
            jax.ShapeDtypeStruct((length, width), BF),
            jax.ShapeDtypeStruct((length * heads, 128), F32),
        ),
        compiler_params=pltpu.CompilerParams(vmem_limit_bytes=40 * 2**20),
        cost_estimate=pl.CostEstimate(
            flops=4 * length * width * (WINDOW + CHUNK),
            bytes_accessed=6 * 2**20,
            transcendentals=length * heads * (WINDOW + CHUNK),
        ),
    )(first, query, keys, values)


def attend_back(first, query, keys, values, logsum, back):
    length, width = query.shape
    heads = width // HEAD_DIM
    vmem = pl.BlockSpec(memory_space=pltpu.VMEM)
    return pl.pallas_call(
        attend_back_kernel,
        in_specs=specs(5),
        out_specs=(vmem, vmem, vmem),
        out_shape=(
            jax.ShapeDtypeStruct((length, width), F32),
            jax.ShapeDtypeStruct(keys.shape, F32),
            jax.ShapeDtypeStruct(values.shape, F32),
        ),
        compiler_params=pltpu.CompilerParams(vmem_limit_bytes=40 * 2**20),
        cost_estimate=pl.CostEstimate(
            flops=10 * length * width * (WINDOW + CHUNK),
            bytes_accessed=8 * 2**20,
            transcendentals=length * heads * (WINDOW + CHUNK),
        ),
    )(first, query, keys, values, logsum, back)


def total_ty(block):
    rows = block.shape[0] // 2
    return block[:rows] + swap(block[rows:].astype(BF), "ty").astype(F32)


def total_dp(block, earlier=None):
    block = block.astype(BF)
    if earlier is not None:
        block, earlier = lax.optimization_barrier((block, earlier))
    return lax.psum(block, "dp"), earlier


def core_total(mine, other):
    return mine + swap(other.astype(BF), "tx").astype(F32)


def per_device(
    tokens,
    cotangent,
    entry_gain,
    query_weight,
    key_weight,
    value_weight,
    query_scale,
    key_scale,
    output_weight,
    mixed_gain,
    feed_gain,
    gate_weight,
    up_weight,
    down_weight,
    final_gain,
):
    tx = lax.axis_index("tx")
    ty = lax.axis_index("ty")
    quarter = tx * 2 + ty
    share, width = tokens.shape
    share //= 2
    query_cols = query_weight.shape[1]
    part = key_weight.shape[1]
    hidden_cols = gate_weight.shape[1]
    places = lax.axis_size("tx") * lax.axis_size("ty")

    gains_own = jnp.stack([entry_gain, mixed_gain, feed_gain, final_gain])
    gains = jnp.concatenate([gains_own, swap(gains_own, "ty")], axis=1)

    def to_rows(array):
        mine = lax.dynamic_slice_in_dim(array, ty * share, share, 0)
        sent = lax.dynamic_slice_in_dim(array, (1 - ty) * share, share, 0)
        return jnp.concatenate([mine, swap(sent, "ty")], axis=1)

    def from_rows(array):
        return ordered(ty, array[:, :width], swap(array[:, width:], "ty"))

    residual = to_rows(tokens).astype(F32)

    entry = jnp.concatenate([query_weight, key_weight, value_weight], axis=1)
    feed = jnp.concatenate([gate_weight, up_weight], axis=1)
    entry_peer = swap(entry, "ty")
    entry_own = jnp.concatenate([entry, entry_peer], axis=0)
    entry_own, residual, feed_half, output_start = lax.optimization_barrier(
        (entry_own, residual, half_of(feed), output_weight)
    )
    entry_other = swap(entry_own, "tx")
    out_peer = swap(output_start, "ty")
    feed_direct = swap(feed_half, "ty")
    out_peer, feed_direct, entry_other, down_half, cotangent = lax.optimization_barrier(
        (out_peer, feed_direct, entry_other, half_of(down_weight), cotangent)
    )
    out_own = jnp.concatenate([output_weight, out_peer], axis=1)
    out_other = swap(out_own, "tx")
    feed_own = jnp.concatenate([feed, relay(feed_direct)], axis=0)
    feed_other = swap(feed_own, "tx")
    down_own = jnp.concatenate([down_weight, relay(swap(down_half, "ty"))], axis=1)
    down_other = swap(down_own, "tx")
    incoming = to_rows(cotangent).astype(F32)

    pair_own = entry_own[:, query_cols:]
    pair_other = entry_other[:, query_cols:]
    query_w = jnp.concatenate([entry_own[:, :query_cols], entry_other[:, :query_cols]], axis=1)
    key_w = ordered(tx, pair_own[:, :part], pair_other[:, :part], axis=1)
    value_w = ordered(tx, pair_own[:, part:], pair_other[:, part:], axis=1)
    pair_w = jnp.concatenate([key_w, value_w], axis=1)
    out_w = jnp.concatenate([out_own, out_other], axis=0)
    down_w = jnp.concatenate([down_own, down_other], axis=0)

    normed, factor_one = norm_forward(residual, gains[0])
    normed = normed.astype(BF)
    pair_raw = mm(normed, pair_w)
    key_raw = pair_raw[:, :HEAD_DIM]
    cosine, sine = rotary_tables(quarter * share + jnp.arange(share, dtype=jnp.int32))
    key_rot, key_pull = jax.vjp(
        partial(head_prepare, cosine=cosine, sine=sine), key_raw[:, None, :], key_scale
    )
    pair_low = jnp.concatenate([key_rot[:, 0, :], pair_raw[:, HEAD_DIM:]], axis=1).astype(BF)
    ahead = [(i, i + 1) for i in range(places - 1)]
    before = lax.ppermute(pair_low, ("tx", "ty"), ahead)
    query_raw = mm(normed, query_w)
    heads = query_raw.shape[1] // HEAD_DIM
    query_rot, query_pull = jax.vjp(
        partial(head_prepare, cosine=cosine, sine=sine),
        query_raw.reshape(share, heads, HEAD_DIM),
        query_scale,
    )
    query_low = query_rot.astype(BF).reshape(share, heads * HEAD_DIM)
    window = jnp.concatenate([before, pair_low], axis=0)
    keys, values = window[:, :HEAD_DIM], window[:, HEAD_DIM:]
    first = quarter.reshape(1).astype(jnp.int32)
    attended, logsum = attend(first, query_low, keys, values)

    mixed = mm(attended, out_w)
    mixed_normed, factor_two = norm_forward(mixed, gains[1])
    hidden = residual + mixed_normed
    fed, factor_three = norm_forward(hidden, gains[2])
    fed = fed.astype(BF)
    hc = hidden_cols
    gate_up_own = mm(fed, feed_own)
    gate_up_other = mm(fed, feed_other)
    inner_own, pull_own = jax.vjp(gated_gelu, gate_up_own[:, :hc], gate_up_own[:, hc:])
    inner_other, pull_other = jax.vjp(gated_gelu, gate_up_other[:, :hc], gate_up_other[:, hc:])
    inner_own = inner_own.astype(BF)
    inner_other = inner_other.astype(BF)
    down = mm(jnp.concatenate([inner_own, inner_other], axis=1), down_w)
    down_normed, factor_four = norm_forward(down, gains[3])
    block_output = from_rows((hidden + down_normed).astype(BF))

    back_down, final_gain_part = norm_backward(down, factor_four, gains[3], incoming)
    back_down = back_down.astype(BF)
    down_total = core_total(mm_tn(back_down, inner_own), mm_tn(back_down, inner_other))
    back_own = jnp.concatenate(pull_own(mm_nt(back_down, down_own)), axis=1).astype(BF)
    back_other = jnp.concatenate(pull_other(mm_nt(back_down, down_other)), axis=1).astype(BF)
    back_own, back_other, down_total = lax.optimization_barrier((back_own, back_other, down_total))
    down_part = total_ty(down_total)
    feed_total = core_total(mm_tn(fed, back_own), mm_tn(fed, back_other))
    back_fed = mm_nt(back_own, feed_own) + mm_nt(back_other, feed_other)
    back_three, feed_gain_part = norm_backward(hidden, factor_three, gains[2], back_fed)
    back_hidden = incoming + back_three
    back_mixed, mixed_gain_part = norm_backward(mixed, factor_two, gains[1], back_hidden)
    back_mixed = back_mixed.astype(BF)
    qc = query_cols
    out_total = core_total(mm_tn(back_mixed, attended[:, :qc]), mm_tn(back_mixed, attended[:, qc:]))
    back_attended = mm_nt(back_mixed, out_w).astype(BF)
    back_attended, down_part, feed_total = lax.optimization_barrier(
        (back_attended, down_part, feed_total)
    )
    down_gradient, _ = total_dp(down_part)
    feed_part = total_ty(feed_total)
    back_query_rot, key_part, value_part = attend_back(
        first, query_low, keys, values, logsum, back_attended
    )
    back_pair = jnp.concatenate([key_part, value_part], axis=1)
    returned = lax.ppermute(
        back_pair[:WINDOW].astype(BF), ("tx", "ty"), [(j, i) for i, j in ahead]
    )
    back_query_raw, query_scale_part = query_pull(
        back_query_rot.reshape(share, heads, HEAD_DIM)
    )
    query_back = back_query_raw.reshape(share, heads * HEAD_DIM).astype(BF)
    back_pair = back_pair[WINDOW:] + returned.astype(F32)
    back_key_raw, key_scale_part = key_pull(back_pair[:, None, :HEAD_DIM])
    key_back = back_key_raw[:, 0, :].astype(BF)
    value_back = back_pair[:, HEAD_DIM:].astype(BF)
    query_back, key_back, value_back, feed_part = lax.optimization_barrier(
        (query_back, key_back, value_back, feed_part)
    )
    feed_gradient, down_gradient = total_dp(feed_part, down_gradient)

    def columns(index, block):
        return jnp.concatenate(
            [
                block,
                lax.dynamic_slice_in_dim(key_back, index * part, part, 1),
                lax.dynamic_slice_in_dim(value_back, index * part, part, 1),
            ],
            axis=1,
        )

    entry_total = core_total(
        mm_tn(normed, columns(tx, query_back[:, :qc])),
        mm_tn(normed, columns(1 - tx, query_back[:, qc:])),
    )
    last_gradient, feed_gradient = total_dp(
        total_ty(jnp.concatenate([entry_total, out_total], axis=1)), feed_gradient
    )
    down_gradient = down_gradient.astype(F32)
    feed_gradient = feed_gradient.astype(F32)
    last_gradient = last_gradient.astype(F32)
    entry_gradient = last_gradient[:, : qc + 2 * part]
    out_gradient = last_gradient[:, qc + 2 * part :]
    back_normed = mm_nt(query_back, query_w) + mm_nt(
        jnp.concatenate([key_back, value_back], axis=1), pair_w
    )
    back_entry, entry_gain_part = norm_backward(residual, factor_one, gains[0], back_normed)
    tokens_gradient = from_rows(back_hidden + back_entry)

    gain_parts = jnp.stack([entry_gain_part, mixed_gain_part, feed_gain_part, final_gain_part])
    gain_parts = ordered(ty, gain_parts[:, :width], gain_parts[:, width:], axis=1)
    gain_totals, query_scale_gradient, key_scale_gradient = lax.psum(
        (gain_parts, query_scale_part, key_scale_part), ("dp", "tx", "ty")
    )
    mine = lax.dynamic_slice_in_dim(gain_totals, ty * width, width, 1)
    return (
        block_output,
        tokens_gradient,
        mine[0],
        entry_gradient[:, :qc],
        entry_gradient[:, qc : qc + part],
        entry_gradient[:, qc + part :],
        query_scale_gradient,
        key_scale_gradient,
        out_gradient.T,
        mine[1],
        mine[2],
        feed_gradient[:, :hc],
        feed_gradient[:, hc:],
        down_gradient.T,
        mine[3],
    )


def solution(mesh):
    in_specs = (
        P(("dp", "tx"), "ty"),
        P(("dp", "tx"), "ty"),
        P("ty"),
        P("ty", "tx"),
        P("ty", "tx"),
        P("ty", "tx"),
        P(),
        P(),
        P("tx", "ty"),
        P("ty"),
        P("ty"),
        P("ty", "tx"),
        P("ty", "tx"),
        P("tx", "ty"),
        P("ty"),
    )
    out_specs = (
        P(("dp", "tx"), "ty"),
        P(("dp", "tx"), "ty"),
        P("ty"),
        P("ty", "tx"),
        P("ty", "tx"),
        P("ty", "tx"),
        P(),
        P(),
        P("tx", "ty"),
        P("ty"),
        P("ty"),
        P("ty", "tx"),
        P("ty", "tx"),
        P("tx", "ty"),
        P("ty"),
    )
    return jax.shard_map(
        per_device, mesh=mesh, in_specs=in_specs, out_specs=out_specs, check_vma=False
    )
```

```python
from functools import partial

import jax
import jax.numpy as jnp
from jax import lax
from jax.experimental import pallas as pl
from jax.experimental.pallas import tpu as pltpu
from jax.sharding import PartitionSpec as P

HEAD_DIM = 256
WINDOW = 512
CHUNK = 128
EPS = 1e-06
MASKED = -1e30
BF = jnp.bfloat16
F32 = jnp.float32


def mm(a, b):
    return jnp.dot(a, b, preferred_element_type=F32)


def mm_nt(a, b):
    return lax.dot_general(a, b, (((1,), (1,)), ((), ())), preferred_element_type=F32)


def mm_tn(a, b):
    return lax.dot_general(a, b, (((0,), (0,)), ((), ())), preferred_element_type=F32)


def swap(value, axis):
    return lax.ppermute(value, axis, [(0, 1), (1, 0)])


def swap_dp(value, bit):
    n = lax.axis_size("dp")
    return lax.ppermute(value, "dp", [(i, i ^ (1 << bit)) for i in range(n)])


def ordered(flag, mine, other, axis=0):
    return jnp.where(
        flag == 0,
        jnp.concatenate([mine, other], axis=axis),
        jnp.concatenate([other, mine], axis=axis),
    )


def half_of(block):
    half = block.shape[0] // 2
    return lax.dynamic_slice_in_dim(block, (lax.axis_index("dp") % 2) * half, half, 0)


def relay(direct):
    return ordered(lax.axis_index("dp") % 2, direct, swap_dp(direct, 0))


def rotary_tables(places):
    half = HEAD_DIM // 2
    inverse = 10000.0 ** (-(jnp.arange(half, dtype=F32) * 2.0) / HEAD_DIM)
    angles = places.astype(F32)[:, None] * inverse[None, :]
    return (jnp.cos(angles)[:, None, :], jnp.sin(angles)[:, None, :])


def rotate(value, cosine, sine):
    half = value.shape[-1] // 2
    first = value[..., :half]
    second = value[..., half:]
    return jnp.concatenate(
        [first * cosine - second * sine, second * cosine + first * sine], axis=-1
    )


def head_prepare(raw, gain, cosine, sine):
    factor = lax.rsqrt(jnp.mean(raw * raw, axis=-1, keepdims=True) + EPS)
    return rotate(raw * factor * (1.0 + gain), cosine, sine)


def gated_gelu(gate, upper):
    return jax.nn.gelu(gate, approximate=True) * upper


def norm_forward(value, gain):
    factor = lax.rsqrt(jnp.mean(value * value, axis=1, keepdims=True) + EPS)
    return (value * factor * (1.0 + gain), factor)


def norm_backward(value, factor, gain, incoming):
    weighted = incoming * (1.0 + gain)
    inner = jnp.mean(value * weighted, axis=1, keepdims=True)
    back_value = weighted * factor - value * factor**3 * inner
    back_gain = jnp.sum(incoming * value * factor, axis=0)
    return (back_value, back_gain)


def band(first_ref, start, heads):
    rows = heads * CHUNK
    span = WINDOW + CHUNK
    place = lax.broadcasted_iota(jnp.int32, (rows, span), 0) % CHUNK
    key = lax.broadcasted_iota(jnp.int32, (rows, span), 1)
    lowest = jnp.where(first_ref[0] > 0, 0, WINDOW - start)
    return (key > place) & (key <= place + WINDOW) & (key >= lowest)


def stack_heads(ref, start, heads):
    return jnp.concatenate(
        [ref[start : start + CHUNK, h * HEAD_DIM : (h + 1) * HEAD_DIM] for h in range(heads)],
        axis=0,
    )


def attend_kernel(first_ref, query_ref, keys_ref, values_ref, out_ref, logsum_ref):
    length, width = query_ref.shape
    heads = width // HEAD_DIM
    factor = HEAD_DIM ** (-0.5)
    for start in range(0, length, CHUNK):
        query = stack_heads(query_ref, start, heads)
        keys = keys_ref[start : start + WINDOW + CHUNK, :]
        values = values_ref[start : start + WINDOW + CHUNK, :]
        scores = jnp.where(band(first_ref, start, heads), mm_nt(query, keys) * factor, MASKED)
        peak = jnp.max(scores, axis=1, keepdims=True)
        raised = jnp.exp(scores - peak)
        mass = jnp.sum(raised, axis=1, keepdims=True)
        shares = (raised / mass).astype(BF)
        out = mm(shares, values).astype(BF)
        logsum_ref[start * heads : (start + CHUNK) * heads, :] = jnp.broadcast_to(
            peak + jnp.log(mass), (heads * CHUNK, 128)
        )
        for h in range(heads):
            out_ref[start : start + CHUNK, h * HEAD_DIM : (h + 1) * HEAD_DIM] = out[
                h * CHUNK : (h + 1) * CHUNK, :
            ]


def attend_back_kernel(
    first_ref, query_ref, keys_ref, values_ref, logsum_ref, back_ref, dq_ref, dk_ref, dv_ref
):
    length, width = query_ref.shape
    heads = width // HEAD_DIM
    factor = HEAD_DIM ** (-0.5)
    dk_ref[...] = jnp.zeros_like(dk_ref)
    dv_ref[...] = jnp.zeros_like(dv_ref)
    for start in range(0, length, CHUNK):
        span = slice(start, start + WINDOW + CHUNK)
        query = stack_heads(query_ref, start, heads)
        back = stack_heads(back_ref, start, heads)
        keys = keys_ref[span, :]
        values = values_ref[span, :]
        scores = jnp.where(band(first_ref, start, heads), mm_nt(query, keys) * factor, MASKED)
        logsum = logsum_ref[start * heads : (start + CHUNK) * heads, :][:, :1]
        exact = jnp.exp(scores - logsum)
        back_shares = mm_nt(back, values)
        inner = jnp.sum(exact * back_shares, axis=1, keepdims=True)
        back_scores = (exact * (back_shares - inner)).astype(BF)
        dq = mm(back_scores, keys) * factor
        dk_ref[span, :] += mm_tn(back_scores, query) * factor
        dv_ref[span, :] += mm_tn(exact.astype(BF), back)
        for h in range(heads):
            dq_ref[start : start + CHUNK, h * HEAD_DIM : (h + 1) * HEAD_DIM] = dq[
                h * CHUNK : (h + 1) * CHUNK, :
            ]


def specs(n):
    vmem = pl.BlockSpec(memory_space=pltpu.VMEM)
    return [pl.BlockSpec(memory_space=pltpu.SMEM)] + [vmem] * n


def attend(first, query, keys, values):
    length, width = query.shape
    heads = width // HEAD_DIM
    vmem = pl.BlockSpec(memory_space=pltpu.VMEM)
    return pl.pallas_call(
        attend_kernel,
        in_specs=specs(3),
        out_specs=(vmem, vmem),
        out_shape=(
            jax.ShapeDtypeStruct((length, width), BF),
            jax.ShapeDtypeStruct((length * heads, 128), F32),
        ),
        compiler_params=pltpu.CompilerParams(vmem_limit_bytes=40 * 2**20),
        cost_estimate=pl.CostEstimate(
            flops=4 * length * width * (WINDOW + CHUNK),
            bytes_accessed=6 * 2**20,
            transcendentals=length * heads * (WINDOW + CHUNK),
        ),
    )(first, query, keys, values)


def attend_back(first, query, keys, values, logsum, back):
    length, width = query.shape
    heads = width // HEAD_DIM
    vmem = pl.BlockSpec(memory_space=pltpu.VMEM)
    return pl.pallas_call(
        attend_back_kernel,
        in_specs=specs(5),
        out_specs=(vmem, vmem, vmem),
        out_shape=(
            jax.ShapeDtypeStruct((length, width), F32),
            jax.ShapeDtypeStruct(keys.shape, F32),
            jax.ShapeDtypeStruct(values.shape, F32),
        ),
        compiler_params=pltpu.CompilerParams(vmem_limit_bytes=40 * 2**20),
        cost_estimate=pl.CostEstimate(
            flops=10 * length * width * (WINDOW + CHUNK),
            bytes_accessed=8 * 2**20,
            transcendentals=length * heads * (WINDOW + CHUNK),
        ),
    )(first, query, keys, values, logsum, back)


def total_ty(block):
    rows = block.shape[0] // 2
    return block[:rows] + swap(block[rows:].astype(BF), "ty").astype(F32)


def dp_bits():
    count = lax.axis_size("dp")
    assert count & (count - 1) == 0
    return list(range(count.bit_length() - 1))


def dp_blocks(block):
    count = lax.axis_size("dp")
    return block.reshape(count, block.shape[0] // count, block.shape[1])


def halve(parts, bit):
    half = parts.shape[0] // 2
    flag = (lax.axis_index("dp") >> bit) & 1
    kept = lax.dynamic_slice_in_dim(parts, flag * half, half, 0)
    sent = lax.dynamic_slice_in_dim(parts, (1 - flag) * half, half, 0).astype(BF)
    return kept + swap_dp(sent, bit).astype(F32)


def double(parts, bit):
    return ordered((lax.axis_index("dp") >> bit) & 1, parts, swap_dp(parts, bit))


def doubled(parts, bits):
    parts = parts.astype(BF)
    for bit in reversed(bits):
        parts = double(parts, bit)
    return parts.astype(F32).reshape(-1, parts.shape[-1])


def total_all(value):
    value = value + swap(value, "tx")
    value = value + swap(value, "ty")
    for bit in dp_bits():
        value = value + swap_dp(value, bit)
    return value


def core_total(mine, other):
    return mine + swap(other.astype(BF), "tx").astype(F32)


def per_device(
    tokens,
    cotangent,
    entry_gain,
    query_weight,
    key_weight,
    value_weight,
    query_scale,
    key_scale,
    output_weight,
    mixed_gain,
    feed_gain,
    gate_weight,
    up_weight,
    down_weight,
    final_gain,
):
    tx = lax.axis_index("tx")
    ty = lax.axis_index("ty")
    quarter = tx * 2 + ty
    share, width = tokens.shape
    share //= 2
    query_cols = query_weight.shape[1]
    part = key_weight.shape[1]
    hidden_cols = gate_weight.shape[1]
    places = lax.axis_size("tx") * lax.axis_size("ty")

    gains_own = jnp.stack([entry_gain, mixed_gain, feed_gain, final_gain])
    gains = jnp.concatenate([gains_own, swap(gains_own, "ty")], axis=1)

    def to_rows(array):
        mine = lax.dynamic_slice_in_dim(array, ty * share, share, 0)
        sent = lax.dynamic_slice_in_dim(array, (1 - ty) * share, share, 0)
        return jnp.concatenate([mine, swap(sent, "ty")], axis=1)

    def from_rows(array):
        return ordered(ty, array[:, :width], swap(array[:, width:], "ty"))

    residual = to_rows(tokens).astype(F32)

    entry = jnp.concatenate([query_weight, key_weight, value_weight], axis=1)
    feed = jnp.concatenate([gate_weight, up_weight], axis=1)
    entry_peer = swap(entry, "ty")
    entry_own = jnp.concatenate([entry, entry_peer], axis=0)
    entry_own, residual, feed_half, output_start = lax.optimization_barrier(
        (entry_own, residual, half_of(feed), output_weight)
    )
    entry_other = swap(entry_own, "tx")
    out_peer = swap(output_start, "ty")
    feed_direct = swap(feed_half, "ty")
    out_peer, feed_direct, down_half, cotangent = lax.optimization_barrier(
        (out_peer, feed_direct, half_of(down_weight), cotangent)
    )
    out_own = jnp.concatenate([output_weight, out_peer], axis=1)
    out_other = swap(out_own, "tx")
    feed_own = jnp.concatenate([feed, relay(feed_direct)], axis=0)
    feed_other = swap(feed_own, "tx")
    down_own = jnp.concatenate([down_weight, relay(swap(down_half, "ty"))], axis=1)
    down_other = swap(down_own, "tx")
    incoming = to_rows(cotangent).astype(F32)

    pair_own = entry_own[:, query_cols:]
    pair_other = entry_other[:, query_cols:]
    query_w = jnp.concatenate([entry_own[:, :query_cols], entry_other[:, :query_cols]], axis=1)
    key_w = ordered(tx, pair_own[:, :part], pair_other[:, :part], axis=1)
    value_w = ordered(tx, pair_own[:, part:], pair_other[:, part:], axis=1)
    pair_w = jnp.concatenate([key_w, value_w], axis=1)
    out_w = jnp.concatenate([out_own, out_other], axis=0)
    down_w = jnp.concatenate([down_own, down_other], axis=0)

    normed, factor_one = norm_forward(residual, gains[0])
    normed = normed.astype(BF)
    pair_raw = mm(normed, pair_w)
    key_raw = pair_raw[:, :HEAD_DIM]
    cosine, sine = rotary_tables(quarter * share + jnp.arange(share, dtype=jnp.int32))
    key_rot, key_pull = jax.vjp(
        partial(head_prepare, cosine=cosine, sine=sine), key_raw[:, None, :], key_scale
    )
    pair_low = jnp.concatenate([key_rot[:, 0, :], pair_raw[:, HEAD_DIM:]], axis=1).astype(BF)
    ahead = [(i, i + 1) for i in range(places - 1)]
    before = lax.ppermute(pair_low, ("tx", "ty"), ahead)
    query_raw = mm(normed, query_w)
    heads = query_raw.shape[1] // HEAD_DIM
    query_rot, query_pull = jax.vjp(
        partial(head_prepare, cosine=cosine, sine=sine),
        query_raw.reshape(share, heads, HEAD_DIM),
        query_scale,
    )
    query_low = query_rot.astype(BF).reshape(share, heads * HEAD_DIM)
    window = jnp.concatenate([before, pair_low], axis=0)
    keys, values = window[:, :HEAD_DIM], window[:, HEAD_DIM:]
    first = quarter.reshape(1).astype(jnp.int32)
    attended, logsum = attend(first, query_low, keys, values)

    mixed = mm(attended, out_w)
    mixed_normed, factor_two = norm_forward(mixed, gains[1])
    hidden = residual + mixed_normed
    fed, factor_three = norm_forward(hidden, gains[2])
    fed = fed.astype(BF)
    hc = hidden_cols
    gate_up_own = mm(fed, feed_own)
    gate_up_other = mm(fed, feed_other)
    inner_own, pull_own = jax.vjp(gated_gelu, gate_up_own[:, :hc], gate_up_own[:, hc:])
    inner_other, pull_other = jax.vjp(gated_gelu, gate_up_other[:, :hc], gate_up_other[:, hc:])
    inner_own = inner_own.astype(BF)
    inner_other = inner_other.astype(BF)
    down = mm(jnp.concatenate([inner_own, inner_other], axis=1), down_w)
    down_normed, factor_four = norm_forward(down, gains[3])
    block_output = from_rows((hidden + down_normed).astype(BF))

    back_down, final_gain_part = norm_backward(down, factor_four, gains[3], incoming)
    back_down = back_down.astype(BF)
    down_total = core_total(mm_tn(back_down, inner_own), mm_tn(back_down, inner_other))
    back_own = jnp.concatenate(pull_own(mm_nt(back_down, down_own)), axis=1).astype(BF)
    back_other = jnp.concatenate(pull_other(mm_nt(back_down, down_other)), axis=1).astype(BF)
    back_own, back_other, down_total = lax.optimization_barrier((back_own, back_other, down_total))
    down_part = total_ty(down_total)
    gate_total = core_total(mm_tn(fed, back_own[:, :hc]), mm_tn(fed, back_other[:, :hc]))
    up_total = core_total(mm_tn(fed, back_own[:, hc:]), mm_tn(fed, back_other[:, hc:]))
    back_fed = mm_nt(back_own, feed_own) + mm_nt(back_other, feed_other)
    back_three, feed_gain_part = norm_backward(hidden, factor_three, gains[2], back_fed)
    back_hidden = incoming + back_three
    back_mixed, mixed_gain_part = norm_backward(mixed, factor_two, gains[1], back_hidden)
    back_mixed = back_mixed.astype(BF)
    qc = query_cols
    out_total = core_total(mm_tn(back_mixed, attended[:, :qc]), mm_tn(back_mixed, attended[:, qc:]))
    back_attended = mm_nt(back_mixed, out_w).astype(BF)
    bits = dp_bits()
    back_attended, down_part, gate_total, up_total = lax.optimization_barrier(
        (back_attended, down_part, gate_total, up_total)
    )
    down_part = dp_blocks(down_part)
    gate_part = total_ty(gate_total)
    back_query_rot, key_part, value_part = attend_back(
        first, query_low, keys, values, logsum, back_attended
    )
    for bit in bits[:1]:
        down_part = halve(down_part, bit)
    back_query_rot, key_part, value_part, gate_part, down_part = lax.optimization_barrier(
        (back_query_rot, key_part, value_part, gate_part, down_part)
    )
    up_part = total_ty(up_total)
    for bit in bits[1:]:
        down_part = halve(down_part, bit)
    back_pair = jnp.concatenate([key_part, value_part], axis=1)
    returned = lax.ppermute(
        back_pair[:WINDOW].astype(BF), ("tx", "ty"), [(j, i) for i, j in ahead]
    )
    back_query_raw, query_scale_part = query_pull(
        back_query_rot.reshape(share, heads, HEAD_DIM)
    )
    query_back = back_query_raw.reshape(share, heads * HEAD_DIM).astype(BF)
    back_pair = back_pair[WINDOW:] + returned.astype(F32)
    back_key_raw, key_scale_part = key_pull(back_pair[:, None, :HEAD_DIM])
    key_back = back_key_raw[:, 0, :].astype(BF)
    value_back = back_pair[:, HEAD_DIM:].astype(BF)
    query_back, key_back, value_back, up_part, down_part = lax.optimization_barrier(
        (query_back, key_back, value_back, up_part, down_part)
    )
    out_part = total_ty(out_total)
    feed_part = dp_blocks(jnp.concatenate([gate_part, up_part, out_part], axis=1))
    down_gradient = doubled(down_part, bits)
    for bit in bits:
        feed_part = halve(feed_part, bit)
    feed_gradient = doubled(feed_part, bits)

    def columns(index, block):
        return jnp.concatenate(
            [
                block,
                lax.dynamic_slice_in_dim(key_back, index * part, part, 1),
                lax.dynamic_slice_in_dim(value_back, index * part, part, 1),
            ],
            axis=1,
        )

    entry_total = core_total(
        mm_tn(normed, columns(tx, query_back[:, :qc])),
        mm_tn(normed, columns(1 - tx, query_back[:, qc:])),
    )
    entry_part = dp_blocks(total_ty(entry_total))
    for bit in bits:
        entry_part = halve(entry_part, bit)
    entry_gradient = doubled(entry_part, bits)
    out_gradient = feed_gradient[:, 2 * hc :]
    back_normed = mm_nt(query_back, query_w) + mm_nt(
        jnp.concatenate([key_back, value_back], axis=1), pair_w
    )
    back_entry, entry_gain_part = norm_backward(residual, factor_one, gains[0], back_normed)
    row_gradient = back_hidden + back_entry
    tokens_gradient = ordered(
        ty, row_gradient[:, :width], swap(row_gradient[:, width:].astype(BF), "ty").astype(F32)
    )

    gain_parts = jnp.stack([entry_gain_part, mixed_gain_part, feed_gain_part, final_gain_part])
    gain_parts = ordered(ty, gain_parts[:, :width], gain_parts[:, width:], axis=1)
    scale_parts = jnp.stack([query_scale_part, key_scale_part])
    joined = total_all(
        jnp.concatenate([gain_parts.reshape(-1), scale_parts.reshape(-1)]).reshape(-1, 128)
    ).reshape(-1)
    gain_totals = joined[: gain_parts.size].reshape(gain_parts.shape)
    query_scale_gradient, key_scale_gradient = joined[gain_parts.size :].reshape(2, HEAD_DIM)
    mine = lax.dynamic_slice_in_dim(gain_totals, ty * width, width, 1)
    return (
        block_output,
        tokens_gradient,
        mine[0],
        entry_gradient[:, :qc],
        entry_gradient[:, qc : qc + part],
        entry_gradient[:, qc + part :],
        query_scale_gradient,
        key_scale_gradient,
        out_gradient.T,
        mine[1],
        mine[2],
        feed_gradient[:, :hc],
        feed_gradient[:, hc : 2 * hc],
        down_gradient.T,
        mine[3],
    )


def solution(mesh):
    in_specs = (
        P(("dp", "tx"), "ty"),
        P(("dp", "tx"), "ty"),
        P("ty"),
        P("ty", "tx"),
        P("ty", "tx"),
        P("ty", "tx"),
        P(),
        P(),
        P("tx", "ty"),
        P("ty"),
        P("ty"),
        P("ty", "tx"),
        P("ty", "tx"),
        P("tx", "ty"),
        P("ty"),
    )
    out_specs = (
        P(("dp", "tx"), "ty"),
        P(("dp", "tx"), "ty"),
        P("ty"),
        P("ty", "tx"),
        P("ty", "tx"),
        P("ty", "tx"),
        P(),
        P(),
        P("tx", "ty"),
        P("ty"),
        P("ty"),
        P("ty", "tx"),
        P("ty", "tx"),
        P("tx", "ty"),
        P("ty"),
    )
    return jax.shard_map(
        per_device, mesh=mesh, in_specs=in_specs, out_specs=out_specs, check_vma=False
    )
```

```python
from functools import partial

import jax
import jax.numpy as jnp
from jax import lax
from jax.experimental import pallas as pl
from jax.experimental.pallas import tpu as pltpu
from jax.sharding import PartitionSpec as P

HEAD_DIM = 256
WINDOW = 512
CHUNK = 128
EPS = 1e-06
MASKED = -1e30
BF = jnp.bfloat16
F32 = jnp.float32


def mm(a, b):
    return jnp.dot(a, b, preferred_element_type=F32)


def mm_nt(a, b):
    return lax.dot_general(a, b, (((1,), (1,)), ((), ())), preferred_element_type=F32)


def mm_tn(a, b):
    return lax.dot_general(a, b, (((0,), (0,)), ((), ())), preferred_element_type=F32)


def swap(value, axis):
    return lax.ppermute(value, axis, [(0, 1), (1, 0)])


def swap_dp(value, bit):
    n = lax.axis_size("dp")
    return lax.ppermute(value, "dp", [(i, i ^ (1 << bit)) for i in range(n)])


def ordered(flag, mine, other, axis=0):
    return jnp.where(
        flag == 0,
        jnp.concatenate([mine, other], axis=axis),
        jnp.concatenate([other, mine], axis=axis),
    )


def half_of(block):
    half = block.shape[0] // 2
    return lax.dynamic_slice_in_dim(block, (lax.axis_index("dp") % 2) * half, half, 0)


def relay(direct):
    return ordered(lax.axis_index("dp") % 2, direct, swap_dp(direct, 0))


def rotary_tables(places):
    half = HEAD_DIM // 2
    inverse = 10000.0 ** (-(jnp.arange(half, dtype=F32) * 2.0) / HEAD_DIM)
    angles = places.astype(F32)[:, None] * inverse[None, :]
    return (jnp.cos(angles)[:, None, :], jnp.sin(angles)[:, None, :])


def rotate(value, cosine, sine):
    half = value.shape[-1] // 2
    first = value[..., :half]
    second = value[..., half:]
    return jnp.concatenate(
        [first * cosine - second * sine, second * cosine + first * sine], axis=-1
    )


def head_prepare(raw, gain, cosine, sine):
    factor = lax.rsqrt(jnp.mean(raw * raw, axis=-1, keepdims=True) + EPS)
    return rotate(raw * factor * (1.0 + gain), cosine, sine)


def gated_gelu(gate, upper):
    return jax.nn.gelu(gate, approximate=True) * upper


def norm_forward(value, gain):
    factor = lax.rsqrt(jnp.mean(value * value, axis=1, keepdims=True) + EPS)
    return (value * factor * (1.0 + gain), factor)


def norm_backward(value, factor, gain, incoming):
    weighted = incoming * (1.0 + gain)
    inner = jnp.mean(value * weighted, axis=1, keepdims=True)
    back_value = weighted * factor - value * factor**3 * inner
    back_gain = jnp.sum(incoming * value * factor, axis=0)
    return (back_value, back_gain)


def band(first_ref, start, heads):
    rows = heads * CHUNK
    span = WINDOW + CHUNK
    place = lax.broadcasted_iota(jnp.int32, (rows, span), 0) % CHUNK
    key = lax.broadcasted_iota(jnp.int32, (rows, span), 1)
    lowest = jnp.where(first_ref[0] > 0, 0, WINDOW - start)
    return (key > place) & (key <= place + WINDOW) & (key >= lowest)


def stack_heads(ref, start, heads):
    return jnp.concatenate(
        [ref[start : start + CHUNK, h * HEAD_DIM : (h + 1) * HEAD_DIM] for h in range(heads)],
        axis=0,
    )


def attend_kernel(first_ref, query_ref, keys_ref, values_ref, out_ref, logsum_ref):
    length, width = query_ref.shape
    heads = width // HEAD_DIM
    factor = HEAD_DIM ** (-0.5)
    for start in range(0, length, CHUNK):
        query = stack_heads(query_ref, start, heads)
        keys = keys_ref[start : start + WINDOW + CHUNK, :]
        values = values_ref[start : start + WINDOW + CHUNK, :]
        scores = jnp.where(band(first_ref, start, heads), mm_nt(query, keys) * factor, MASKED)
        peak = jnp.max(scores, axis=1, keepdims=True)
        raised = jnp.exp(scores - peak)
        mass = jnp.sum(raised, axis=1, keepdims=True)
        shares = (raised / mass).astype(BF)
        out = mm(shares, values).astype(BF)
        logsum_ref[start * heads : (start + CHUNK) * heads, :] = jnp.broadcast_to(
            peak + jnp.log(mass), (heads * CHUNK, 128)
        )
        for h in range(heads):
            out_ref[start : start + CHUNK, h * HEAD_DIM : (h + 1) * HEAD_DIM] = out[
                h * CHUNK : (h + 1) * CHUNK, :
            ]


def attend_back_kernel(
    first_ref, query_ref, keys_ref, values_ref, logsum_ref, back_ref, dq_ref, dk_ref, dv_ref
):
    length, width = query_ref.shape
    heads = width // HEAD_DIM
    factor = HEAD_DIM ** (-0.5)
    dk_ref[...] = jnp.zeros_like(dk_ref)
    dv_ref[...] = jnp.zeros_like(dv_ref)
    for start in range(0, length, CHUNK):
        span = slice(start, start + WINDOW + CHUNK)
        query = stack_heads(query_ref, start, heads)
        back = stack_heads(back_ref, start, heads)
        keys = keys_ref[span, :]
        values = values_ref[span, :]
        scores = jnp.where(band(first_ref, start, heads), mm_nt(query, keys) * factor, MASKED)
        logsum = logsum_ref[start * heads : (start + CHUNK) * heads, :][:, :1]
        exact = jnp.exp(scores - logsum)
        back_shares = mm_nt(back, values)
        inner = jnp.sum(exact * back_shares, axis=1, keepdims=True)
        back_scores = (exact * (back_shares - inner)).astype(BF)
        dq = mm(back_scores, keys) * factor
        dk_ref[span, :] += mm_tn(back_scores, query) * factor
        dv_ref[span, :] += mm_tn(exact.astype(BF), back)
        for h in range(heads):
            dq_ref[start : start + CHUNK, h * HEAD_DIM : (h + 1) * HEAD_DIM] = dq[
                h * CHUNK : (h + 1) * CHUNK, :
            ]


def specs(n):
    vmem = pl.BlockSpec(memory_space=pltpu.VMEM)
    return [pl.BlockSpec(memory_space=pltpu.SMEM)] + [vmem] * n


def attend(first, query, keys, values):
    length, width = query.shape
    heads = width // HEAD_DIM
    vmem = pl.BlockSpec(memory_space=pltpu.VMEM)
    return pl.pallas_call(
        attend_kernel,
        in_specs=specs(3),
        out_specs=(vmem, vmem),
        out_shape=(
            jax.ShapeDtypeStruct((length, width), BF),
            jax.ShapeDtypeStruct((length * heads, 128), F32),
        ),
        compiler_params=pltpu.CompilerParams(vmem_limit_bytes=40 * 2**20),
        cost_estimate=pl.CostEstimate(
            flops=4 * length * width * (WINDOW + CHUNK),
            bytes_accessed=6 * 2**20,
            transcendentals=length * heads * (WINDOW + CHUNK),
        ),
    )(first, query, keys, values)


def attend_back(first, query, keys, values, logsum, back):
    length, width = query.shape
    heads = width // HEAD_DIM
    vmem = pl.BlockSpec(memory_space=pltpu.VMEM)
    return pl.pallas_call(
        attend_back_kernel,
        in_specs=specs(5),
        out_specs=(vmem, vmem, vmem),
        out_shape=(
            jax.ShapeDtypeStruct((length, width), F32),
            jax.ShapeDtypeStruct(keys.shape, F32),
            jax.ShapeDtypeStruct(values.shape, F32),
        ),
        compiler_params=pltpu.CompilerParams(vmem_limit_bytes=40 * 2**20),
        cost_estimate=pl.CostEstimate(
            flops=10 * length * width * (WINDOW + CHUNK),
            bytes_accessed=8 * 2**20,
            transcendentals=length * heads * (WINDOW + CHUNK),
        ),
    )(first, query, keys, values, logsum, back)


def total_ty(block):
    rows = block.shape[0] // 2
    return block[:rows] + swap(block[rows:].astype(BF), "ty").astype(F32)


def dp_bits():
    count = lax.axis_size("dp")
    assert count & (count - 1) == 0
    return list(range(count.bit_length() - 1))


def dp_blocks(block):
    count = lax.axis_size("dp")
    return block.reshape(count, block.shape[0] // count, block.shape[1])


def halve(parts, bit):
    half = parts.shape[0] // 2
    flag = (lax.axis_index("dp") >> bit) & 1
    kept = lax.dynamic_slice_in_dim(parts, flag * half, half, 0)
    sent = lax.dynamic_slice_in_dim(parts, (1 - flag) * half, half, 0).astype(BF)
    return kept + swap_dp(sent, bit).astype(F32)


def double(parts, bit):
    return ordered((lax.axis_index("dp") >> bit) & 1, parts, swap_dp(parts, bit))


def doubled(parts, bits):
    parts = parts.astype(BF)
    for bit in reversed(bits):
        parts = double(parts, bit)
    return parts.astype(F32).reshape(-1, parts.shape[-1])


def total_all(value):
    value = value + swap(value, "tx")
    value = value + swap(value, "ty")
    for bit in dp_bits():
        value = value + swap_dp(value, bit)
    return value


def core_total(mine, other):
    return mine + swap(other.astype(BF), "tx").astype(F32)


def per_device(
    tokens,
    cotangent,
    entry_gain,
    query_weight,
    key_weight,
    value_weight,
    query_scale,
    key_scale,
    output_weight,
    mixed_gain,
    feed_gain,
    gate_weight,
    up_weight,
    down_weight,
    final_gain,
):
    tx = lax.axis_index("tx")
    ty = lax.axis_index("ty")
    quarter = tx * 2 + ty
    share, width = tokens.shape
    share //= 2
    query_cols = query_weight.shape[1]
    part = key_weight.shape[1]
    hidden_cols = gate_weight.shape[1]
    places = lax.axis_size("tx") * lax.axis_size("ty")

    gains_own = jnp.stack([entry_gain, mixed_gain, feed_gain, final_gain])
    gains = jnp.concatenate([gains_own, swap(gains_own, "ty")], axis=1)

    def to_rows(array):
        mine = lax.dynamic_slice_in_dim(array, ty * share, share, 0)
        sent = lax.dynamic_slice_in_dim(array, (1 - ty) * share, share, 0)
        return jnp.concatenate([mine, swap(sent, "ty")], axis=1)

    def from_rows(array):
        return ordered(ty, array[:, :width], swap(array[:, width:], "ty"))

    residual = to_rows(tokens).astype(F32)

    entry = jnp.concatenate([query_weight, key_weight, value_weight], axis=1)
    feed = jnp.concatenate([gate_weight, up_weight], axis=1)
    entry_peer = swap(entry, "ty")
    entry_own = jnp.concatenate([entry, entry_peer], axis=0)
    entry_own, residual, feed_half, output_start = lax.optimization_barrier(
        (entry_own, residual, half_of(feed), output_weight)
    )
    entry_other = swap(entry_own, "tx")
    out_peer = swap(output_start, "ty")
    feed_direct = swap(feed_half, "ty")
    pair_own = entry_own[:, query_cols:]
    pair_other = entry_other[:, query_cols:]
    query_w = jnp.concatenate([entry_own[:, :query_cols], entry_other[:, :query_cols]], axis=1)
    key_w = ordered(tx, pair_own[:, :part], pair_other[:, :part], axis=1)
    value_w = ordered(tx, pair_own[:, part:], pair_other[:, part:], axis=1)
    pair_w = jnp.concatenate([key_w, value_w], axis=1)

    normed, factor_one = norm_forward(residual, gains[0])
    normed = normed.astype(BF)
    pair_raw = mm(normed, pair_w)
    key_raw = pair_raw[:, :HEAD_DIM]
    cosine, sine = rotary_tables(quarter * share + jnp.arange(share, dtype=jnp.int32))
    key_rot, key_pull = jax.vjp(
        partial(head_prepare, cosine=cosine, sine=sine), key_raw[:, None, :], key_scale
    )
    pair_low = jnp.concatenate([key_rot[:, 0, :], pair_raw[:, HEAD_DIM:]], axis=1).astype(BF)
    ahead = [(i, i + 1) for i in range(places - 1)]
    before = lax.ppermute(pair_low, ("tx", "ty"), ahead)
    query_raw = mm(normed, query_w)
    heads = query_raw.shape[1] // HEAD_DIM
    query_rot, query_pull = jax.vjp(
        partial(head_prepare, cosine=cosine, sine=sine),
        query_raw.reshape(share, heads, HEAD_DIM),
        query_scale,
    )
    query_low = query_rot.astype(BF).reshape(share, heads * HEAD_DIM)
    out_peer, feed_direct, down_half, cotangent, query_low = lax.optimization_barrier(
        (out_peer, feed_direct, half_of(down_weight), cotangent, query_low)
    )
    out_own = jnp.concatenate([output_weight, out_peer], axis=1)
    out_other = swap(out_own, "tx")
    feed_own = jnp.concatenate([feed, relay(feed_direct)], axis=0)
    feed_other = swap(feed_own, "tx")
    down_own = jnp.concatenate([down_weight, relay(swap(down_half, "ty"))], axis=1)
    down_other = swap(down_own, "tx")
    incoming = to_rows(cotangent).astype(F32)
    out_w = jnp.concatenate([out_own, out_other], axis=0)
    down_w = jnp.concatenate([down_own, down_other], axis=0)

    window = jnp.concatenate([before, pair_low], axis=0)
    keys, values = window[:, :HEAD_DIM], window[:, HEAD_DIM:]
    first = quarter.reshape(1).astype(jnp.int32)
    attended, logsum = attend(first, query_low, keys, values)

    mixed = mm(attended, out_w)
    mixed_normed, factor_two = norm_forward(mixed, gains[1])
    hidden = residual + mixed_normed
    fed, factor_three = norm_forward(hidden, gains[2])
    fed = fed.astype(BF)
    hc = hidden_cols
    gate_up_own = mm(fed, feed_own)
    gate_up_other = mm(fed, feed_other)
    inner_own, pull_own = jax.vjp(gated_gelu, gate_up_own[:, :hc], gate_up_own[:, hc:])
    inner_other, pull_other = jax.vjp(gated_gelu, gate_up_other[:, :hc], gate_up_other[:, hc:])
    inner_own = inner_own.astype(BF)
    inner_other = inner_other.astype(BF)
    down = mm(jnp.concatenate([inner_own, inner_other], axis=1), down_w)
    down_normed, factor_four = norm_forward(down, gains[3])
    block_output = from_rows((hidden + down_normed).astype(BF))

    back_down, final_gain_part = norm_backward(down, factor_four, gains[3], incoming)
    back_down = back_down.astype(BF)
    down_total = core_total(mm_tn(back_down, inner_own), mm_tn(back_down, inner_other))
    back_own = jnp.concatenate(pull_own(mm_nt(back_down, down_own)), axis=1).astype(BF)
    back_other = jnp.concatenate(pull_other(mm_nt(back_down, down_other)), axis=1).astype(BF)
    back_own, back_other, down_total = lax.optimization_barrier((back_own, back_other, down_total))
    down_part = total_ty(down_total)
    gate_total = core_total(mm_tn(fed, back_own[:, :hc]), mm_tn(fed, back_other[:, :hc]))
    up_total = core_total(mm_tn(fed, back_own[:, hc:]), mm_tn(fed, back_other[:, hc:]))
    back_fed = mm_nt(back_own, feed_own) + mm_nt(back_other, feed_other)
    back_three, feed_gain_part = norm_backward(hidden, factor_three, gains[2], back_fed)
    back_hidden = incoming + back_three
    back_mixed, mixed_gain_part = norm_backward(mixed, factor_two, gains[1], back_hidden)
    back_mixed = back_mixed.astype(BF)
    qc = query_cols
    out_total = core_total(mm_tn(back_mixed, attended[:, :qc]), mm_tn(back_mixed, attended[:, qc:]))
    back_attended = mm_nt(back_mixed, out_w).astype(BF)
    bits = dp_bits()
    back_attended, down_part, gate_total, up_total = lax.optimization_barrier(
        (back_attended, down_part, gate_total, up_total)
    )
    down_part = dp_blocks(down_part)
    gate_part = total_ty(gate_total)
    back_query_rot, key_part, value_part = attend_back(
        first, query_low, keys, values, logsum, back_attended
    )
    for bit in bits[:1]:
        down_part = halve(down_part, bit)
    back_query_rot, key_part, value_part, gate_part, down_part = lax.optimization_barrier(
        (back_query_rot, key_part, value_part, gate_part, down_part)
    )
    up_part = total_ty(up_total)
    for bit in bits[1:]:
        down_part = halve(down_part, bit)
    back_pair = jnp.concatenate([key_part, value_part], axis=1)
    returned = lax.ppermute(
        back_pair[:WINDOW].astype(BF), ("tx", "ty"), [(j, i) for i, j in ahead]
    )
    back_query_raw, query_scale_part = query_pull(
        back_query_rot.reshape(share, heads, HEAD_DIM)
    )
    query_back = back_query_raw.reshape(share, heads * HEAD_DIM).astype(BF)
    back_pair = back_pair[WINDOW:] + returned.astype(F32)
    back_key_raw, key_scale_part = key_pull(back_pair[:, None, :HEAD_DIM])
    key_back = back_key_raw[:, 0, :].astype(BF)
    value_back = back_pair[:, HEAD_DIM:].astype(BF)
    query_back, key_back, value_back, up_part, down_part = lax.optimization_barrier(
        (query_back, key_back, value_back, up_part, down_part)
    )
    out_part = total_ty(out_total)
    feed_part = dp_blocks(jnp.concatenate([gate_part, up_part, out_part], axis=1))
    down_gradient = doubled(down_part, bits)
    for bit in bits:
        feed_part = halve(feed_part, bit)
    feed_gradient = doubled(feed_part, bits)

    def columns(index, block):
        return jnp.concatenate(
            [
                block,
                lax.dynamic_slice_in_dim(key_back, index * part, part, 1),
                lax.dynamic_slice_in_dim(value_back, index * part, part, 1),
            ],
            axis=1,
        )

    entry_total = core_total(
        mm_tn(normed, columns(tx, query_back[:, :qc])),
        mm_tn(normed, columns(1 - tx, query_back[:, qc:])),
    )
    query_back, key_back, value_back, entry_total = lax.optimization_barrier(
        (query_back, key_back, value_back, entry_total)
    )
    entry_part = dp_blocks(total_ty(entry_total))
    for bit in bits:
        entry_part = halve(entry_part, bit)
    entry_gradient = doubled(entry_part, bits)
    out_gradient = feed_gradient[:, 2 * hc :]
    back_normed = mm_nt(query_back, query_w) + mm_nt(
        jnp.concatenate([key_back, value_back], axis=1), pair_w
    )
    back_entry, entry_gain_part = norm_backward(residual, factor_one, gains[0], back_normed)
    row_gradient = back_hidden + back_entry
    tokens_gradient = ordered(
        ty, row_gradient[:, :width], swap(row_gradient[:, width:].astype(BF), "ty").astype(F32)
    )

    gain_parts = jnp.stack([entry_gain_part, mixed_gain_part, feed_gain_part, final_gain_part])
    gain_parts = ordered(ty, gain_parts[:, :width], gain_parts[:, width:], axis=1)
    scale_parts = jnp.stack([query_scale_part, key_scale_part])
    joined = total_all(
        jnp.concatenate([gain_parts.reshape(-1), scale_parts.reshape(-1)]).reshape(-1, 128)
    ).reshape(-1)
    gain_totals = joined[: gain_parts.size].reshape(gain_parts.shape)
    query_scale_gradient, key_scale_gradient = joined[gain_parts.size :].reshape(2, HEAD_DIM)
    mine = lax.dynamic_slice_in_dim(gain_totals, ty * width, width, 1)
    return (
        block_output,
        tokens_gradient,
        mine[0],
        entry_gradient[:, :qc],
        entry_gradient[:, qc : qc + part],
        entry_gradient[:, qc + part :],
        query_scale_gradient,
        key_scale_gradient,
        out_gradient.T,
        mine[1],
        mine[2],
        feed_gradient[:, :hc],
        feed_gradient[:, hc : 2 * hc],
        down_gradient.T,
        mine[3],
    )


def solution(mesh):
    in_specs = (
        P(("dp", "tx"), "ty"),
        P(("dp", "tx"), "ty"),
        P("ty"),
        P("ty", "tx"),
        P("ty", "tx"),
        P("ty", "tx"),
        P(),
        P(),
        P("tx", "ty"),
        P("ty"),
        P("ty"),
        P("ty", "tx"),
        P("ty", "tx"),
        P("tx", "ty"),
        P("ty"),
    )
    out_specs = (
        P(("dp", "tx"), "ty"),
        P(("dp", "tx"), "ty"),
        P("ty"),
        P("ty", "tx"),
        P("ty", "tx"),
        P("ty", "tx"),
        P(),
        P(),
        P("tx", "ty"),
        P("ty"),
        P("ty"),
        P("ty", "tx"),
        P("ty", "tx"),
        P("tx", "ty"),
        P("ty"),
    )
    return jax.shard_map(
        per_device, mesh=mesh, in_specs=in_specs, out_specs=out_specs, check_vma=False
    )
```
